32 devices in a mesh: seq: 16 (over z, x, core), head: 2 (over y).
Axes of the slice: x: 2, y: 2, z: 4, core: 2. Of those that a mesh axis runs over, the one named last changes fastest.
Arguments:
- queries: bfloat16 [11264, 4096], P(('seq', 'head')), may hold values from -64 to 64
- database_rows: bfloat16 [128, 64, 896], P('seq', 'head'), may hold values from -6 to 6
- w_encoder: bfloat16 [896, 896], P('seq'), may hold values from -0.1875 to 0.1875
- w_key: bfloat16 [896, 4096], P(None, 'head'), may hold values from -0.1875 to 0.1875
- w_value: bfloat16 [896, 4096], P(None, 'head'), may hold values from -0.1875 to 0.1875
- neighbour_ids: int32 [176, 2], replicated, may hold values from 0 to 127, as said below
Outputs:
- attended: bfloat16 [11264, 4096], P(('seq', 'head'))
The draws below stay inside these ranges and needn't reach their ends.
Inputs may be any that keep to these rules, and one draw needn't show every extreme that they name: `neighbour_ids`: among the 22 neighbours of the spans of one sequence shard (rows s * 11 onward), at most 2 are entries of any one database shard, and in every shard some database shard holds exactly 2 of them. The same entry may appear more than once.
All inputs are finite; a program needn't handle non-finite values.
Results may differ from the reference program's by a relative error of at most 0.012.
The reference program's roundings to bfloat16 on the way (of `normed`, `encoded` and `probs`) count: a program that leaves them out, or rounds other values in their place, can miss the bound.
Values may be sent and summed in bfloat16 or wider, within the bound.
No kernel may reach another device: no remote copies, remote signals or barrier semaphores. Data moves between devices by JAX's collectives and lax.ppermute only.
A program may use at most 64 MiB of HBM per device.

```python
import jax
import jax.numpy as jnp
from jax import lax

D = 4096
HEADS = 32
HEAD_DIM = 128
ENC = 896
SPAN = 64
NBR_LEN = 64
K_NBR = 2
DB_DEV = 8
TOKENS = 11264
SPANS = 176
DB = 128
NBR_DEV = 22
CAP = 2


def draw_queries(key, part):
    first = jax.random.fold_in(jax.random.fold_in(key, 11), 0)
    drawn = jax.random.normal(first, (TOKENS, D), jnp.float32)
    return jnp.clip(drawn, -64.0, 64.0).astype(jnp.bfloat16)


def draw_neighbour_ids(key, part):
    shard_owner_count = DB // DB_DEV
    block_count = SPANS * K_NBR // NBR_DEV
    slot_grand_total = shard_owner_count * CAP
    first, second, third, fourth = jax.random.split(jax.random.fold_in(key, 23), 4)
    popular_position = jax.random.permutation(first, shard_owner_count).astype(jnp.int32)
    slot_shard_owner = jnp.repeat(jnp.arange(shard_owner_count, dtype=jnp.int32), CAP)
    extra_reward = (shard_owner_count - popular_position[slot_shard_owner]) * (2 * (2 ** 20 // shard_owner_count))
    extra_reward = extra_reward + jnp.where(popular_position[slot_shard_owner] == 0, 2 ** 23, 0)
    random_jitter = jax.random.randint(second, (block_count, slot_grand_total), 0, 2 ** 20)
    ranking_score = (random_jitter + extra_reward[None, :]) * slot_grand_total + jnp.arange(slot_grand_total, dtype=jnp.int32)[None, :]
    picked_score, picked = lax.top_k(ranking_score, NBR_DEV)
    owners = slot_shard_owner[picked]
    shuffle_score = jax.random.randint(third, (block_count, NBR_DEV), 0, 2 ** 20) * NBR_DEV + jnp.arange(NBR_DEV, dtype=jnp.int32)[None, :]
    order = jnp.argsort(shuffle_score, axis=1)
    owners = jnp.take_along_axis(owners, order, axis=1)
    local_entry = jax.random.randint(fourth, (block_count, NBR_DEV), 0, DB_DEV)
    return (owners * DB_DEV + local_entry).reshape(SPANS, K_NBR).astype(jnp.int32)


def shard_levels(own_key, dims, shards, least, high):
    loudness, own = 1.0, jax.random.fold_in(own_key, 6)
    for position, shards_of in shards:
        heights = jnp.exp(jax.random.uniform(jax.random.fold_in(own, position), (shards_of,), jnp.float32, least / len(shards), high / len(shards)))
        loudness = loudness * jnp.repeat(heights, dims[position] // shards_of).reshape([-1 if axis == position else 1 for axis in range(len(dims))])
    return loudness


def gaussian(key, extent, deviation, most, pieces=(), kind=jnp.bfloat16):
    entries = deviation * jax.random.normal(key, extent, jnp.float32)
    if pieces:
        entries = entries * shard_levels(key, extent, pieces, -0.22, 0.18)
    return jnp.clip(entries, -most, most).astype(kind)


def setup_inputs(seed: int = 0) -> dict:
    arg_keys = jax.random.split(jax.random.key(seed), 7)
    return {
        "queries": draw_queries(jax.random.fold_in(arg_keys[6], 71), 0),
        "database_rows": gaussian(arg_keys[1], (DB, NBR_LEN, ENC), 1.0, 6.0, ((0, 16), (1, 2))),
        "w_encoder": gaussian(arg_keys[2], (ENC, ENC), ENC ** -0.5, 0.1875, ((0, 16),)),
        "w_key": gaussian(arg_keys[3], (ENC, D), ENC ** -0.5, 0.1875, ((1, 2),)),
        "w_value": gaussian(arg_keys[4], (ENC, D), ENC ** -0.5, 0.1875, ((1, 2),)),
        "neighbour_ids": draw_neighbour_ids(jax.random.fold_in(arg_keys[6], 71), 0),
    }


def encode(raw_rows, w_encoder):
    values_in = raw_rows.astype(jnp.float32)
    mean_square = lax.optimization_barrier(jnp.mean(values_in * values_in, axis=-1, keepdims=True))
    normed = (values_in * lax.rsqrt(mean_square + 1e-06)).astype(jnp.bfloat16)
    summed = jnp.dot(normed.reshape(-1, values_in.shape[-1]), w_encoder, preferred_element_type=jnp.float32)
    return (values_in + jax.nn.silu(summed.reshape(values_in.shape))).astype(jnp.bfloat16)

def attend(query_block, key_block, value_block):
    scores = jnp.einsum('cqhd,ckhd->chqk', query_block.astype(jnp.float32), key_block.astype(jnp.float32)) * HEAD_DIM ** (-0.5)
    highest = lax.optimization_barrier(jnp.max(scores, axis=-1, keepdims=True))
    weights = jnp.exp(scores - highest)
    probs = (weights / lax.optimization_barrier(jnp.sum(weights, axis=-1, keepdims=True))).astype(jnp.bfloat16)
    mixed = jnp.einsum('chqk,ckhd->cqhd', probs.astype(jnp.float32), value_block.astype(jnp.float32))
    return mixed.astype(jnp.bfloat16)

def reference(queries, database_rows, w_encoder, w_key, w_value, neighbour_ids):
    encoded = encode(database_rows, w_encoder)
    flat_rows = encoded.reshape(-1, ENC)
    all_keys = jnp.dot(flat_rows, w_key, preferred_element_type=jnp.float32).astype(jnp.bfloat16).reshape(DB, NBR_LEN, D)
    all_values = jnp.dot(flat_rows, w_value, preferred_element_type=jnp.float32).astype(jnp.bfloat16).reshape(DB, NBR_LEN, D)
    query_spans = queries.reshape(SPANS, 1, SPAN, HEADS, HEAD_DIM)

    def one_span(inputs):
        query_block, entry_ids = inputs
        key_block = all_keys[entry_ids].reshape(1, K_NBR * NBR_LEN, HEADS, HEAD_DIM)
        value_block = all_values[entry_ids].reshape(1, K_NBR * NBR_LEN, HEADS, HEAD_DIM)
        return attend(query_block, key_block, value_block)
    attended = lax.map(one_span, (query_spans, neighbour_ids))
    return attended.reshape(TOKENS, D)
```

```python
import functools

import jax
import jax.numpy as jnp
from jax import lax
from jax.experimental import pallas as pl
from jax.experimental.pallas import tpu as pltpu
from jax.sharding import PartitionSpec as P

HEAD_DIM = 128
SPAN = 64
NBR_LEN = 64
K_NBR = 2
DB_DEV = 8
KEYS = K_NBR * NBR_LEN
SHARERS = 4
BLOCK_HEADS = 4
EXP_SCALE = HEAD_DIM ** (-0.5) * 1.4426950408889634


def xor_permute(x, bits):
    count = lax.axis_size("seq")
    return lax.ppermute(x, "seq", [(i, i ^ bits) for i in range(count)])


def shift_heads(x, shift):
    count = lax.axis_size("head")
    return lax.ppermute(x, "head", [(i, (i + shift) % count) for i in range(count)])


def after(x, *others):
    return lax.optimization_barrier((x, *others))[0]


def encode_kernel(raw_ref, w_ref, out_ref):
    values_in = raw_ref[...].astype(jnp.float32)
    mean_square = jnp.mean(values_in * values_in, axis=-1, keepdims=True)
    normed = (values_in * lax.rsqrt(mean_square + 1e-06)).astype(jnp.bfloat16)
    summed = jnp.dot(normed, w_ref[...], preferred_element_type=jnp.float32)
    out_ref[...] = (values_in + summed / (1.0 + jnp.exp(-summed))).astype(jnp.bfloat16)


def encode_rows(raw_rows, w_encoder):
    flops = 2 * raw_rows.size * w_encoder.shape[1]
    return pl.pallas_call(
        encode_kernel,
        out_shape=jax.ShapeDtypeStruct(raw_rows.shape, raw_rows.dtype),
        compiler_params=pltpu.CompilerParams(vmem_limit_bytes=24 << 20),
        cost_estimate=pl.CostEstimate(
            flops=flops, bytes_accessed=4 * raw_rows.size + 2 * w_encoder.size, transcendentals=raw_rows.size
        ),
        name="encode",
    )(raw_rows, w_encoder)


def attend_heads(keys_of, values_of, q_ref, o_ref, qf_ref, of_ref, offset):
    rows, wide = q_ref.shape
    spans = qf_ref.shape[0] // SPAN
    qf_ref[pl.ds(offset, rows), :] = q_ref[...]
    heads = [slice(at, at + HEAD_DIM) for at in range(0, wide, HEAD_DIM)]
    places = [(slice(span * SPAN, (span + 1) * SPAN), span, cols) for cols in heads for span in range(spans)]
    scores = [
        lax.dot_general(
            qf_ref[lines, cols], keys_of(span, cols), (((1,), (1,)), ((), ())), preferred_element_type=jnp.float32
        )
        for lines, span, cols in places
    ]
    probs = []
    for score in scores:
        highest = jnp.max(score, axis=-1, keepdims=True)
        raised = jnp.exp2(score * EXP_SCALE - highest * EXP_SCALE)
        probs.append((raised * (1.0 / jnp.sum(raised, axis=-1, keepdims=True))).astype(jnp.bfloat16))
    for (lines, span, cols), prob in zip(places, probs):
        mixed = jnp.dot(prob, values_of(span, cols), preferred_element_type=jnp.float32)
        of_ref[lines, cols] = mixed.astype(jnp.bfloat16)
    o_ref[...] = of_ref[pl.ds(offset, rows), :]


def span_rows(refs, span, cols):
    tokens = KEYS // len(refs)
    return jnp.concatenate([ref[span * tokens:(span + 1) * tokens, cols] for ref in refs], axis=0)


def make_parts(enc_refs, w, made_ref):
    for part, enc_ref in enumerate(enc_refs):
        made_ref[part] = jnp.dot(enc_ref[...], w, preferred_element_type=jnp.float32).astype(jnp.bfloat16)
    return [made_ref.at[part] for part in range(len(enc_refs))]


def own_kernel(parts, info_ref, *refs):
    enc_refs = refs[:parts - 1]
    first_k, first_v, wk_ref, wv_ref, q_ref, o_ref, ks_ref, vs_ref, qf_ref, of_ref = refs[parts - 1:]
    k_refs = [first_k, *make_parts(enc_refs, wk_ref[...], ks_ref)]
    v_refs = [first_v, *make_parts(enc_refs, wv_ref[...], vs_ref)]
    attend_heads(
        functools.partial(span_rows, k_refs), functools.partial(span_rows, v_refs),
        q_ref, o_ref, qf_ref, of_ref, pl.multiple_of(info_ref[0], 16),
    )


def sent_kernel(parts, info_ref, *refs):
    enc_refs, wk_refs, wv_refs = refs[:parts], refs[parts:parts + SHARERS], refs[parts + SHARERS:parts + 2 * SHARERS]
    q_ref, _, o_ref, ks_ref, vs_ref, qf_ref, of_ref = refs[parts + 2 * SHARERS:]
    for piece in range(SHARERS):
        @pl.when(pl.program_id(0) == piece)
        def _(piece=piece):
            k_refs = make_parts(enc_refs, wk_refs[piece][...], ks_ref)
            v_refs = make_parts(enc_refs, wv_refs[piece][...], vs_ref)
            attend_heads(
                functools.partial(span_rows, k_refs), functools.partial(span_rows, v_refs),
                q_ref, o_ref, qf_ref, of_ref, pl.multiple_of(info_ref[0], 16),
            )


def cost(encoded, rows, columns):
    made = sum(part.size for part in encoded)
    return pl.CostEstimate(
        flops=4 * made * columns + 4 * rows * KEYS * columns,
        bytes_accessed=2 * made + 4 * rows * columns + 4 * encoded[0].shape[1] * columns,
        transcendentals=rows * KEYS * columns // HEAD_DIM,
    )


def scratch(parts, part_rows, spans, wide):
    return [pltpu.VMEM((parts, part_rows, wide), jnp.bfloat16)] * 2 + [
        pltpu.VMEM((spans * SPAN, wide), jnp.bfloat16)
    ] * 2


def attend_own(info, encoded, first_keys, first_values, w_key, w_value, queries, spans):
    rows, columns = queries.shape[0], w_key.shape[1]
    part_rows, enc_width = encoded[0].shape
    wide = min(BLOCK_HEADS * HEAD_DIM, columns)
    whole = pl.BlockSpec((part_rows, enc_width), lambda i, s: (0, 0))
    lines = pl.BlockSpec((part_rows, wide), lambda i, s: (0, i))
    weights = pl.BlockSpec((enc_width, wide), lambda i, s: (0, i))
    block = pl.BlockSpec((rows, wide), lambda i, s: (0, s[1] * (columns // wide) + i))
    return pl.pallas_call(
        functools.partial(own_kernel, len(encoded) + 1),
        grid_spec=pltpu.PrefetchScalarGridSpec(
            num_scalar_prefetch=1,
            grid=(columns // wide,),
            in_specs=[whole] * len(encoded) + [lines, lines, weights, weights, block],
            out_specs=block,
            scratch_shapes=scratch(len(encoded), part_rows, spans, wide),
        ),
        out_shape=jax.ShapeDtypeStruct(queries.shape, queries.dtype),
        compiler_params=pltpu.CompilerParams(vmem_limit_bytes=32 << 20),
        cost_estimate=cost(encoded, rows, columns),
        name="attend_own",
    )(info, *encoded, first_keys, first_values, w_key, w_value, queries)


def attend_sent(info, encoded, key_pieces, value_pieces, queries, out, spans):
    parts, rows = len(encoded), queries.shape[0]
    part_rows, enc_width = encoded[0].shape
    wide = key_pieces[0].shape[1]
    whole = pl.BlockSpec((part_rows, enc_width), lambda i, s: (0, 0))
    weights = pl.BlockSpec((enc_width, wide), lambda i, s: (0, 0))
    block = pl.BlockSpec((rows, wide), lambda i, s: (0, s[1 + i]))
    return pl.pallas_call(
        functools.partial(sent_kernel, parts),
        grid_spec=pltpu.PrefetchScalarGridSpec(
            num_scalar_prefetch=1,
            grid=(SHARERS,),
            in_specs=[whole] * parts + [weights] * (2 * SHARERS) + [block, pl.BlockSpec(memory_space=pl.ANY)],
            out_specs=block,
            scratch_shapes=scratch(parts, part_rows, spans, wide),
        ),
        out_shape=jax.ShapeDtypeStruct(out.shape, out.dtype),
        input_output_aliases={parts + 2 * SHARERS + 2: 0},
        compiler_params=pltpu.CompilerParams(vmem_limit_bytes=40 << 20),
        cost_estimate=cost(encoded, rows, SHARERS * wide),
        name="attend_sent",
    )(info, *encoded, *key_pieces, *value_pieces, queries, out)


def project(rows, weights):
    return jnp.dot(rows, weights, preferred_element_type=jnp.float32).astype(jnp.bfloat16)


def per_device(queries, database_rows, w_encoder, w_key, w_value, neighbour_ids):
    seq_count, head_count = lax.axis_size("seq"), lax.axis_size("head")
    seq_index, head_index = lax.axis_index("seq"), lax.axis_index("head")
    rows, group_cols = queries.shape[0], w_key.shape[1]
    half = seq_count // 2

    top, order = [half, half // 2, half + half // 2], [0, half, half // 2, half + half // 2]
    enc_blocks = jnp.stack([w_encoder, *[xor_permute(w_encoder, bits) for bits in top]])
    top_blocks, bit = enc_blocks, half // 4
    while bit:
        enc_blocks = jnp.concatenate([enc_blocks, xor_permute(enc_blocks, bit)], axis=0)
        order = order + [m ^ bit for m in order]
        bit //= 2
    place = jnp.array([order.index(m) for m in range(seq_count)], jnp.int32)
    place = place[seq_index ^ jnp.arange(seq_count, dtype=jnp.int32)]
    w_full = enc_blocks[place].reshape(-1, w_encoder.shape[1])

    by_shard = neighbour_ids.reshape(seq_count, -1)
    cited_count = by_shard.shape[1]
    cap_count = max(2, (cited_count + seq_count - 1) // seq_count)
    owners = by_shard // DB_DEV
    local_entry = by_shard % DB_DEV
    position = jnp.arange(cited_count, dtype=jnp.int32)
    same_owner = (owners[:, :, None] == owners[:, None, :]) & (
        position[None, None, :] < position[None, :, None]
    )
    earlier = jnp.sum(same_owner.astype(jnp.int32), axis=2)
    slot_index = jnp.arange(cap_count, dtype=jnp.int32)
    matches = (owners == seq_index)[:, None, :] & (earlier[:, None, :] == slot_index[None, :, None])
    source_entry = jnp.sum(jnp.where(matches, local_entry[:, None, :], 0), axis=2)
    entries = after(database_rows[source_entry], top_blocks)
    arrived = lax.all_to_all(entries, "seq", split_axis=0, concat_axis=0, tiled=True)
    flat_arrived = arrived.reshape(-1, arrived.shape[2], arrived.shape[3])
    cited_slot = lax.dynamic_index_in_dim(owners * cap_count + earlier, seq_index, 0, keepdims=False)

    shard_spans = cited_count // K_NBR
    spans = max(-(-(h * rows % SPAN + rows) // SPAN) for h in range(head_count))

    def neighbours_of(head):
        first_span = head * rows // SPAN
        span_ids = jnp.minimum(first_span + jnp.arange(spans, dtype=jnp.int32), shard_spans - 1)
        places = (span_ids[:, None] * K_NBR + jnp.arange(K_NBR, dtype=jnp.int32)).reshape(-1)
        return flat_arrived[cited_slot[places]].reshape(-1, flat_arrived.shape[2])

    received = [
        shift_heads(neighbours_of((head_index + shift) % head_count), shift) for shift in range(1, head_count)
    ]
    kept = neighbours_of(head_index)

    piece_cols = group_cols // SHARERS
    piece_index = ((seq_index >> 1) ^ (seq_index >> 2)) % 2 * 2 + seq_index % 2
    sent = []
    for shift in range(1, head_count):
        shared = []
        for weights, axis_bit in ((w_key, 2), (w_value, 4)):
            first = shift_heads(lax.dynamic_slice_in_dim(weights, piece_index * piece_cols, piece_cols, 1), shift)
            second = xor_permute(first, axis_bit)
            shared.append((first, second, xor_permute(first, 1), xor_permute(after(second, kept), 1)))
        group = (head_index - shift) % head_count
        sent.append((shared, [group * SHARERS + (piece_index ^ mask) for mask in (0, 2, 1, 3)]))

    encoded = [encode_rows(part, w_full) for part in (kept, *received)]
    offset = head_index * rows % SPAN
    framed = rows % 16 != 0
    if framed:
        frame = jnp.zeros((spans * SPAN, queries.shape[1]), queries.dtype)
        queries = lax.dynamic_update_slice_in_dim(frame, queries, offset, 0)
        first_row, offset = offset, jnp.int32(0)
    info = jnp.stack([offset, head_index]).astype(jnp.int32)
    first_keys, first_values = project(encoded[0], w_key), project(encoded[0], w_value)
    out = attend_own(info, encoded[1:], first_keys, first_values, w_key, w_value, queries, spans)
    for (key_pieces, value_pieces), blocks in sent:
        info = jnp.stack([offset, *blocks]).astype(jnp.int32)
        out = attend_sent(info, encoded, key_pieces, value_pieces, queries, out, spans)
    if framed:
        out = lax.dynamic_slice_in_dim(out, first_row, rows, 0)
    return out


def solution(mesh):
    placed = (
        P(("seq", "head"), None),
        P("seq", "head", None),
        P("seq", None),
        P(None, "head"),
        P(None, "head"),
        P(),
    )
    return jax.shard_map(
        per_device, mesh=mesh, in_specs=placed, out_specs=P(("seq", "head"), None), check_vma=False
    )
```

```python
import functools

import jax
import jax.numpy as jnp
from jax import lax
from jax.experimental import pallas as pl
from jax.experimental.pallas import tpu as pltpu
from jax.sharding import PartitionSpec as P

HEAD_DIM = 128
SPAN = 64
NBR_LEN = 64
K_NBR = 2
DB_DEV = 8
KEYS = K_NBR * NBR_LEN
SHARERS = 4
BLOCK_HEADS = 4
EXP_SCALE = HEAD_DIM ** (-0.5) * 1.4426950408889634


def xor_permute(x, bits):
    count = lax.axis_size("seq")
    return lax.ppermute(x, "seq", [(i, i ^ bits) for i in range(count)])


def shift_heads(x, shift):
    count = lax.axis_size("head")
    return lax.ppermute(x, "head", [(i, (i + shift) % count) for i in range(count)])


def after(x, *others):
    return lax.optimization_barrier((x, *others))[0]


def encode_kernel(raw_ref, w_ref, out_ref):
    values_in = raw_ref[...].astype(jnp.float32)
    mean_square = jnp.mean(values_in * values_in, axis=-1, keepdims=True)
    normed = (values_in * lax.rsqrt(mean_square + 1e-06)).astype(jnp.bfloat16)
    summed = jnp.dot(normed, w_ref[...], preferred_element_type=jnp.float32)
    out_ref[...] = (values_in + summed / (1.0 + jnp.exp(-summed))).astype(jnp.bfloat16)


def encode_rows(raw_rows, w_encoder):
    flops = 2 * raw_rows.size * w_encoder.shape[1]
    return pl.pallas_call(
        encode_kernel,
        out_shape=jax.ShapeDtypeStruct(raw_rows.shape, raw_rows.dtype),
        compiler_params=pltpu.CompilerParams(vmem_limit_bytes=24 << 20),
        cost_estimate=pl.CostEstimate(
            flops=flops, bytes_accessed=4 * raw_rows.size + 2 * w_encoder.size, transcendentals=raw_rows.size
        ),
        name="encode",
    )(raw_rows, w_encoder)


def attend_heads(keys_of, values_of, q_ref, o_ref, qf_ref, of_ref, offset):
    rows, wide = q_ref.shape
    spans = qf_ref.shape[0] // SPAN
    qf_ref[pl.ds(offset, rows), :] = q_ref[...]
    heads = [slice(at, at + HEAD_DIM) for at in range(0, wide, HEAD_DIM)]
    places = [(slice(span * SPAN, (span + 1) * SPAN), span, cols) for cols in heads for span in range(spans)]
    scores = [
        lax.dot_general(
            qf_ref[lines, cols], keys_of(span, cols), (((1,), (1,)), ((), ())), preferred_element_type=jnp.float32
        )
        for lines, span, cols in places
    ]
    probs = []
    for score in scores:
        highest = jnp.max(score, axis=-1, keepdims=True)
        raised = jnp.exp2(score * EXP_SCALE - highest * EXP_SCALE)
        probs.append((raised * (1.0 / jnp.sum(raised, axis=-1, keepdims=True))).astype(jnp.bfloat16))
    for (lines, span, cols), prob in zip(places, probs):
        mixed = jnp.dot(prob, values_of(span, cols), preferred_element_type=jnp.float32)
        of_ref[lines, cols] = mixed.astype(jnp.bfloat16)
    o_ref[...] = of_ref[pl.ds(offset, rows), :]


def span_rows(refs, span, cols):
    tokens = KEYS // len(refs)
    return jnp.concatenate([ref[span * tokens:(span + 1) * tokens, cols] for ref in refs], axis=0)


def make_parts(enc_refs, w, made_ref):
    for part, enc_ref in enumerate(enc_refs):
        made_ref[part] = jnp.dot(enc_ref[...], w, preferred_element_type=jnp.float32).astype(jnp.bfloat16)
    return [made_ref.at[part] for part in range(len(enc_refs))]


def own_kernel(parts, info_ref, *refs):
    enc_refs = refs[:parts - 1]
    first_k, first_v, wk_ref, wv_ref, q_ref, o_ref, ks_ref, vs_ref, qf_ref, of_ref = refs[parts - 1:]
    wide = q_ref.shape[1]
    here = pl.ds(pl.multiple_of(pl.program_id(0) * wide, wide), wide)
    k_refs = [first_k.at[:, here], *make_parts(enc_refs, wk_ref[:, here], ks_ref)]
    v_refs = [first_v.at[:, here], *make_parts(enc_refs, wv_ref[:, here], vs_ref)]
    attend_heads(
        functools.partial(span_rows, k_refs), functools.partial(span_rows, v_refs),
        q_ref, o_ref, qf_ref, of_ref, pl.multiple_of(info_ref[0], 16),
    )


def sent_kernel(parts, info_ref, *refs):
    enc_refs, wk_refs, wv_refs = refs[:parts], refs[parts:parts + SHARERS], refs[parts + SHARERS:parts + 2 * SHARERS]
    q_ref, _, o_ref, ks_ref, vs_ref, qf_ref, of_ref = refs[parts + 2 * SHARERS:]
    for piece in range(SHARERS):
        @pl.when(pl.program_id(0) == piece)
        def _(piece=piece):
            k_refs = make_parts(enc_refs, wk_refs[piece][...], ks_ref)
            v_refs = make_parts(enc_refs, wv_refs[piece][...], vs_ref)
            attend_heads(
                functools.partial(span_rows, k_refs), functools.partial(span_rows, v_refs),
                q_ref, o_ref, qf_ref, of_ref, pl.multiple_of(info_ref[0], 16),
            )


def cost(encoded, rows, columns):
    made = sum(part.size for part in encoded)
    return pl.CostEstimate(
        flops=4 * made * columns + 4 * rows * KEYS * columns,
        bytes_accessed=2 * made + 4 * rows * columns + 4 * encoded[0].shape[1] * columns,
        transcendentals=rows * KEYS * columns // HEAD_DIM,
    )


def scratch(parts, part_rows, spans, wide):
    return [pltpu.VMEM((parts, part_rows, wide), jnp.bfloat16)] * 2 + [
        pltpu.VMEM((spans * SPAN, wide), jnp.bfloat16)
    ] * 2


def attend_own(info, encoded, first_keys, first_values, w_key, w_value, queries, spans):
    rows, columns = queries.shape[0], w_key.shape[1]
    part_rows, enc_width = encoded[0].shape
    wide = min(BLOCK_HEADS * HEAD_DIM, columns)
    whole = pl.BlockSpec(memory_space=pltpu.VMEM)
    block = pl.BlockSpec((rows, wide), lambda i, s: (0, s[1] * (columns // wide) + i))
    return pl.pallas_call(
        functools.partial(own_kernel, len(encoded) + 1),
        grid_spec=pltpu.PrefetchScalarGridSpec(
            num_scalar_prefetch=1,
            grid=(columns // wide,),
            in_specs=[whole] * (len(encoded) + 4) + [block],
            out_specs=block,
            scratch_shapes=scratch(len(encoded), part_rows, spans, wide),
        ),
        out_shape=jax.ShapeDtypeStruct(queries.shape, queries.dtype),
        compiler_params=pltpu.CompilerParams(vmem_limit_bytes=32 << 20),
        cost_estimate=cost(encoded, rows, columns),
        name="attend_own",
    )(info, *encoded, first_keys, first_values, w_key, w_value, queries)


def attend_sent(info, encoded, key_pieces, value_pieces, queries, out, spans):
    parts, rows = len(encoded), queries.shape[0]
    part_rows, enc_width = encoded[0].shape
    wide = key_pieces[0].shape[1]
    whole = pl.BlockSpec((part_rows, enc_width), lambda i, s: (0, 0))
    weights = pl.BlockSpec((enc_width, wide), lambda i, s: (0, 0))
    block = pl.BlockSpec((rows, wide), lambda i, s: (0, s[1 + i]))
    return pl.pallas_call(
        functools.partial(sent_kernel, parts),
        grid_spec=pltpu.PrefetchScalarGridSpec(
            num_scalar_prefetch=1,
            grid=(SHARERS,),
            in_specs=[whole] * parts + [weights] * (2 * SHARERS) + [block, pl.BlockSpec(memory_space=pl.ANY)],
            out_specs=block,
            scratch_shapes=scratch(parts, part_rows, spans, wide),
        ),
        out_shape=jax.ShapeDtypeStruct(out.shape, out.dtype),
        input_output_aliases={parts + 2 * SHARERS + 2: 0},
        compiler_params=pltpu.CompilerParams(vmem_limit_bytes=40 << 20),
        cost_estimate=cost(encoded, rows, SHARERS * wide),
        name="attend_sent",
    )(info, *encoded, *key_pieces, *value_pieces, queries, out)


def project(rows, weights):
    return jnp.dot(rows, weights, preferred_element_type=jnp.float32).astype(jnp.bfloat16)


def per_device(queries, database_rows, w_encoder, w_key, w_value, neighbour_ids):
    seq_count, head_count = lax.axis_size("seq"), lax.axis_size("head")
    seq_index, head_index = lax.axis_index("seq"), lax.axis_index("head")
    rows, group_cols = queries.shape[0], w_key.shape[1]
    half = seq_count // 2

    top, order = [half, half // 2, half + half // 2], [0, half, half // 2, half + half // 2]
    enc_blocks = jnp.stack([w_encoder, *[xor_permute(w_encoder, bits) for bits in top]])
    top_blocks, bit = enc_blocks, half // 4
    while bit:
        enc_blocks = jnp.concatenate([enc_blocks, xor_permute(enc_blocks, bit)], axis=0)
        order = order + [m ^ bit for m in order]
        bit //= 2
    place = jnp.array([order.index(m) for m in range(seq_count)], jnp.int32)
    place = place[seq_index ^ jnp.arange(seq_count, dtype=jnp.int32)]
    w_full = enc_blocks[place].reshape(-1, w_encoder.shape[1])

    by_shard = neighbour_ids.reshape(seq_count, -1)
    cited_count = by_shard.shape[1]
    cap_count = max(2, (cited_count + seq_count - 1) // seq_count)
    owners = by_shard // DB_DEV
    local_entry = by_shard % DB_DEV
    position = jnp.arange(cited_count, dtype=jnp.int32)
    same_owner = (owners[:, :, None] == owners[:, None, :]) & (
        position[None, None, :] < position[None, :, None]
    )
    earlier = jnp.sum(same_owner.astype(jnp.int32), axis=2)
    slot_index = jnp.arange(cap_count, dtype=jnp.int32)
    matches = (owners == seq_index)[:, None, :] & (earlier[:, None, :] == slot_index[None, :, None])
    source_entry = jnp.sum(jnp.where(matches, local_entry[:, None, :], 0), axis=2)
    entries = after(database_rows[source_entry], top_blocks)
    arrived = lax.all_to_all(entries, "seq", split_axis=0, concat_axis=0, tiled=True)
    flat_arrived = arrived.reshape(-1, arrived.shape[2], arrived.shape[3])
    cited_slot = lax.dynamic_index_in_dim(owners * cap_count + earlier, seq_index, 0, keepdims=False)

    shard_spans = cited_count // K_NBR
    spans = max(-(-(h * rows % SPAN + rows) // SPAN) for h in range(head_count))

    def neighbours_of(head):
        first_span = head * rows // SPAN
        span_ids = jnp.minimum(first_span + jnp.arange(spans, dtype=jnp.int32), shard_spans - 1)
        places = (span_ids[:, None] * K_NBR + jnp.arange(K_NBR, dtype=jnp.int32)).reshape(-1)
        return flat_arrived[cited_slot[places]].reshape(-1, flat_arrived.shape[2])

    received = [
        shift_heads(neighbours_of((head_index + shift) % head_count), shift) for shift in range(1, head_count)
    ]
    kept = neighbours_of(head_index)

    encoded = [encode_rows(part, w_full) for part in (kept, *received)]
    own_keys, own_values = project(encoded[0], w_key), project(encoded[0], w_value)
    piece_cols = group_cols // SHARERS
    piece_index = ((seq_index >> 1) ^ (seq_index >> 2)) % 2 * 2 + seq_index % 2
    sent = []
    for shift in range(1, head_count):
        shared = []
        for weights, axis_bit in ((w_key, 2), (w_value, 4)):
            first = shift_heads(lax.dynamic_slice_in_dim(weights, piece_index * piece_cols, piece_cols, 1), shift)
            second = xor_permute(first, axis_bit)
            shared.append((first, second, xor_permute(first, 1), xor_permute(after(second, own_values), 1)))
        group = (head_index - shift) % head_count
        sent.append((shared, [group * SHARERS + (piece_index ^ mask) for mask in (0, 2, 1, 3)]))

    offset = head_index * rows % SPAN
    framed = rows % 16 != 0
    if framed:
        frame = jnp.zeros((spans * SPAN, queries.shape[1]), queries.dtype)
        queries = lax.dynamic_update_slice_in_dim(frame, queries, offset, 0)
        first_row, offset = offset, jnp.int32(0)
    info = jnp.stack([offset, head_index]).astype(jnp.int32)
    out = attend_own(info, encoded[1:], own_keys, own_values, w_key, w_value, queries, spans)
    for (key_pieces, value_pieces), blocks in sent:
        info = jnp.stack([offset, *blocks]).astype(jnp.int32)
        out = attend_sent(info, encoded, key_pieces, value_pieces, queries, out, spans)
    if framed:
        out = lax.dynamic_slice_in_dim(out, first_row, rows, 0)
    return out


def solution(mesh):
    placed = (
        P(("seq", "head"), None),
        P("seq", "head", None),
        P("seq", None),
        P(None, "head"),
        P(None, "head"),
        P(),
    )
    return jax.shard_map(
        per_device, mesh=mesh, in_specs=placed, out_specs=P(("seq", "head"), None), check_vma=False
    )
```

```python
import functools

import jax
import jax.numpy as jnp
from jax import lax
from jax.experimental import pallas as pl
from jax.experimental.pallas import tpu as pltpu
from jax.sharding import PartitionSpec as P

HEAD_DIM = 128
SPAN = 64
NBR_LEN = 64
K_NBR = 2
DB_DEV = 8
KEYS = K_NBR * NBR_LEN
SHARERS = 4
BLOCK_HEADS = 4
EXP_SCALE = HEAD_DIM ** (-0.5) * 1.4426950408889634


def xor_permute(x, bits):
    count = lax.axis_size("seq")
    return lax.ppermute(x, "seq", [(i, i ^ bits) for i in range(count)])


def shift_heads(x, shift):
    count = lax.axis_size("head")
    return lax.ppermute(x, "head", [(i, (i + shift) % count) for i in range(count)])


def after(x, *others):
    return lax.optimization_barrier((x, *others))[0]


def encode_kernel(raw_ref, w_ref, out_ref):
    values_in = raw_ref[...].astype(jnp.float32)
    mean_square = jnp.mean(values_in * values_in, axis=-1, keepdims=True)
    normed = (values_in * lax.rsqrt(mean_square + 1e-06)).astype(jnp.bfloat16)
    summed = jnp.dot(normed, w_ref[...], preferred_element_type=jnp.float32)
    out_ref[...] = (values_in + summed / (1.0 + jnp.exp(-summed))).astype(jnp.bfloat16)


def encode_rows(raw_rows, w_encoder):
    flops = 2 * raw_rows.size * w_encoder.shape[1]
    return pl.pallas_call(
        encode_kernel,
        out_shape=jax.ShapeDtypeStruct(raw_rows.shape, raw_rows.dtype),
        compiler_params=pltpu.CompilerParams(vmem_limit_bytes=24 << 20),
        cost_estimate=pl.CostEstimate(
            flops=flops, bytes_accessed=4 * raw_rows.size + 2 * w_encoder.size, transcendentals=raw_rows.size
        ),
        name="encode",
    )(raw_rows, w_encoder)


def attend_heads(keys_of, values_of, q_ref, o_ref, qf_ref, of_ref, offset):
    rows, wide = q_ref.shape
    spans = qf_ref.shape[0] // SPAN
    qf_ref[pl.ds(offset, rows), :] = q_ref[...]
    heads = [slice(at, at + HEAD_DIM) for at in range(0, wide, HEAD_DIM)]
    places = [(slice(span * SPAN, (span + 1) * SPAN), span, cols) for cols in heads for span in range(spans)]
    scores = [
        lax.dot_general(
            qf_ref[lines, cols], keys_of(span, cols), (((1,), (1,)), ((), ())), preferred_element_type=jnp.float32
        )
        for lines, span, cols in places
    ]
    probs = []
    for score in scores:
        highest = jnp.max(score, axis=-1, keepdims=True)
        raised = jnp.exp2(score * EXP_SCALE - highest * EXP_SCALE)
        probs.append((raised * (1.0 / jnp.sum(raised, axis=-1, keepdims=True))).astype(jnp.bfloat16))
    for (lines, span, cols), prob in zip(places, probs):
        mixed = jnp.dot(prob, values_of(span, cols), preferred_element_type=jnp.float32)
        of_ref[lines, cols] = mixed.astype(jnp.bfloat16)
    o_ref[...] = of_ref[pl.ds(offset, rows), :]


def span_rows(refs, span, cols):
    tokens = KEYS // len(refs)
    return jnp.concatenate([ref[span * tokens:(span + 1) * tokens, cols] for ref in refs], axis=0)


def make_parts(enc_refs, w, made_ref):
    for part, enc_ref in enumerate(enc_refs):
        made_ref[part] = jnp.dot(enc_ref[...], w, preferred_element_type=jnp.float32).astype(jnp.bfloat16)
    return [made_ref.at[part] for part in range(len(enc_refs))]


def own_kernel(parts, info_ref, *refs):
    enc_refs = refs[:parts - 1]
    first_k, first_v, wk_ref, wv_ref, q_ref, o_ref, ks_ref, vs_ref, qf_ref, of_ref = refs[parts - 1:]
    wide = q_ref.shape[1]
    here = pl.ds(pl.multiple_of(pl.program_id(0) * wide, wide), wide)
    k_refs = [first_k.at[:, here], *make_parts(enc_refs, wk_ref[:, here], ks_ref)]
    v_refs = [first_v.at[:, here], *make_parts(enc_refs, wv_ref[:, here], vs_ref)]
    attend_heads(
        functools.partial(span_rows, k_refs), functools.partial(span_rows, v_refs),
        q_ref, o_ref, qf_ref, of_ref, pl.multiple_of(info_ref[0], 16),
    )


def sent_kernel(parts, info_ref, *refs):
    enc_refs, wk_refs, wv_refs = refs[:parts], refs[parts:parts + SHARERS], refs[parts + SHARERS:parts + 2 * SHARERS]
    q_ref, _, o_ref, w_ref, sems, ks_ref, vs_ref, qf_ref, of_ref = refs[parts + 2 * SHARERS:]
    step = pl.program_id(0)
    slot = lax.rem(step, 2)

    def fetch(piece, into):
        return [
            pltpu.make_async_copy(source, w_ref.at[into, at], sems.at[into, at])
            for at, source in enumerate((wk_refs[piece], wv_refs[piece]))
        ]

    for piece in range(SHARERS):
        @pl.when(step == max(piece - 1, 0))
        def _(piece=piece):
            for copy in fetch(piece, piece % 2):
                copy.start()
    for copy in fetch(0, slot):
        copy.wait()
    k_refs = make_parts(enc_refs, w_ref[slot, 0], ks_ref)
    v_refs = make_parts(enc_refs, w_ref[slot, 1], vs_ref)
    attend_heads(
        functools.partial(span_rows, k_refs), functools.partial(span_rows, v_refs),
        q_ref, o_ref, qf_ref, of_ref, pl.multiple_of(info_ref[0], 16),
    )


def cost(encoded, rows, columns):
    made = sum(part.size for part in encoded)
    return pl.CostEstimate(
        flops=4 * made * columns + 4 * rows * KEYS * columns,
        bytes_accessed=2 * made + 4 * rows * columns + 4 * encoded[0].shape[1] * columns,
        transcendentals=rows * KEYS * columns // HEAD_DIM,
    )


def scratch(parts, part_rows, spans, wide):
    return [pltpu.VMEM((parts, part_rows, wide), jnp.bfloat16)] * 2 + [
        pltpu.VMEM((spans * SPAN, wide), jnp.bfloat16)
    ] * 2


def attend_own(info, encoded, first_keys, first_values, w_key, w_value, queries, spans):
    rows, columns = queries.shape[0], w_key.shape[1]
    part_rows, enc_width = encoded[0].shape
    wide = min(BLOCK_HEADS * HEAD_DIM, columns)
    whole = pl.BlockSpec(memory_space=pltpu.VMEM)
    block = pl.BlockSpec((rows, wide), lambda i, s: (0, s[1] * (columns // wide) + i))
    return pl.pallas_call(
        functools.partial(own_kernel, len(encoded) + 1),
        grid_spec=pltpu.PrefetchScalarGridSpec(
            num_scalar_prefetch=1,
            grid=(columns // wide,),
            in_specs=[whole] * (len(encoded) + 4) + [block],
            out_specs=block,
            scratch_shapes=scratch(len(encoded), part_rows, spans, wide),
        ),
        out_shape=jax.ShapeDtypeStruct(queries.shape, queries.dtype),
        compiler_params=pltpu.CompilerParams(vmem_limit_bytes=32 << 20),
        cost_estimate=cost(encoded, rows, columns),
        name="attend_own",
    )(info, *encoded, first_keys, first_values, w_key, w_value, queries)


def attend_sent(info, encoded, key_pieces, value_pieces, queries, out, spans):
    parts, rows = len(encoded), queries.shape[0]
    part_rows, enc_width = encoded[0].shape
    wide = key_pieces[0].shape[1]
    whole = pl.BlockSpec((part_rows, enc_width), lambda i, s: (0, 0))
    weights = pl.BlockSpec(memory_space=pl.ANY)
    block = pl.BlockSpec((rows, wide), lambda i, s: (0, s[1 + i]))
    return pl.pallas_call(
        functools.partial(sent_kernel, parts),
        grid_spec=pltpu.PrefetchScalarGridSpec(
            num_scalar_prefetch=1,
            grid=(SHARERS,),
            in_specs=[whole] * parts + [weights] * (2 * SHARERS) + [block, pl.BlockSpec(memory_space=pl.ANY)],
            out_specs=block,
            scratch_shapes=[
                pltpu.VMEM((2, 2, enc_width, wide), jnp.bfloat16), pltpu.SemaphoreType.DMA((2, 2)),
                *scratch(parts, part_rows, spans, wide),
            ],
        ),
        out_shape=jax.ShapeDtypeStruct(out.shape, out.dtype),
        input_output_aliases={parts + 2 * SHARERS + 2: 0},
        compiler_params=pltpu.CompilerParams(vmem_limit_bytes=40 << 20),
        cost_estimate=cost(encoded, rows, SHARERS * wide),
        name="attend_sent",
    )(info, *encoded, *key_pieces, *value_pieces, queries, out)


def project(rows, weights):
    return jnp.dot(rows, weights, preferred_element_type=jnp.float32).astype(jnp.bfloat16)


def per_device(queries, database_rows, w_encoder, w_key, w_value, neighbour_ids):
    seq_count, head_count = lax.axis_size("seq"), lax.axis_size("head")
    seq_index, head_index = lax.axis_index("seq"), lax.axis_index("head")
    rows, group_cols = queries.shape[0], w_key.shape[1]
    half = seq_count // 2

    top, order = [half, half // 2, half + half // 2], [0, half, half // 2, half + half // 2]
    enc_blocks = jnp.stack([w_encoder, *[xor_permute(w_encoder, bits) for bits in top]])
    top_blocks, bit = enc_blocks, half // 4
    while bit:
        enc_blocks = jnp.concatenate([enc_blocks, xor_permute(enc_blocks, bit)], axis=0)
        order = order + [m ^ bit for m in order]
        bit //= 2
    place = jnp.array([order.index(m) for m in range(seq_count)], jnp.int32)
    place = place[seq_index ^ jnp.arange(seq_count, dtype=jnp.int32)]
    w_full = enc_blocks[place].reshape(-1, w_encoder.shape[1])

    by_shard = neighbour_ids.reshape(seq_count, -1)
    cited_count = by_shard.shape[1]
    cap_count = max(2, (cited_count + seq_count - 1) // seq_count)
    owners = by_shard // DB_DEV
    local_entry = by_shard % DB_DEV
    position = jnp.arange(cited_count, dtype=jnp.int32)
    same_owner = (owners[:, :, None] == owners[:, None, :]) & (
        position[None, None, :] < position[None, :, None]
    )
    earlier = jnp.sum(same_owner.astype(jnp.int32), axis=2)
    slot_index = jnp.arange(cap_count, dtype=jnp.int32)
    matches = (owners == seq_index)[:, None, :] & (earlier[:, None, :] == slot_index[None, :, None])
    source_entry = jnp.sum(jnp.where(matches, local_entry[:, None, :], 0), axis=2)
    entries = after(database_rows[source_entry], top_blocks)
    arrived = lax.all_to_all(entries, "seq", split_axis=0, concat_axis=0, tiled=True)
    flat_arrived = arrived.reshape(-1, arrived.shape[2], arrived.shape[3])
    cited_slot = lax.dynamic_index_in_dim(owners * cap_count + earlier, seq_index, 0, keepdims=False)

    shard_spans = cited_count // K_NBR
    spans = max(-(-(h * rows % SPAN + rows) // SPAN) for h in range(head_count))

    def neighbours_of(head):
        first_span = head * rows // SPAN
        span_ids = jnp.minimum(first_span + jnp.arange(spans, dtype=jnp.int32), shard_spans - 1)
        places = (span_ids[:, None] * K_NBR + jnp.arange(K_NBR, dtype=jnp.int32)).reshape(-1)
        return flat_arrived[cited_slot[places]].reshape(-1, flat_arrived.shape[2])

    received = [
        shift_heads(neighbours_of((head_index + shift) % head_count), shift) for shift in range(1, head_count)
    ]
    kept = neighbours_of(head_index)

    encoded = [encode_rows(part, w_full) for part in (kept, *received)]
    own_keys, own_values = project(encoded[0], w_key), project(encoded[0], w_value)
    piece_cols = group_cols // SHARERS
    piece_index = ((seq_index >> 1) ^ (seq_index >> 2)) % 2 * 2 + seq_index % 2
    sent = []
    for shift in range(1, head_count):
        shared = []
        for weights, axis_bit in ((w_key, 2), (w_value, 4)):
            first = shift_heads(lax.dynamic_slice_in_dim(weights, piece_index * piece_cols, piece_cols, 1), shift)
            second = xor_permute(first, axis_bit)
            shared.append((first, second, xor_permute(first, 1), xor_permute(after(second, own_values), 1)))
        group = (head_index - shift) % head_count
        sent.append((shared, [group * SHARERS + (piece_index ^ mask) for mask in (0, 2, 1, 3)]))

    offset = head_index * rows % SPAN
    framed = rows % 16 != 0
    if framed:
        frame = jnp.zeros((spans * SPAN, queries.shape[1]), queries.dtype)
        queries = lax.dynamic_update_slice_in_dim(frame, queries, offset, 0)
        first_row, offset = offset, jnp.int32(0)
    info = jnp.stack([offset, head_index]).astype(jnp.int32)
    out = attend_own(info, encoded[1:], own_keys, own_values, w_key, w_value, queries, spans)
    for (key_pieces, value_pieces), blocks in sent:
        info = jnp.stack([offset, *blocks]).astype(jnp.int32)
        out = attend_sent(info, encoded, key_pieces, value_pieces, queries, out, spans)
    if framed:
        out = lax.dynamic_slice_in_dim(out, first_row, rows, 0)
    return out


def solution(mesh):
    placed = (
        P(("seq", "head"), None),
        P("seq", "head", None),
        P("seq", None),
        P(None, "head"),
        P(None, "head"),
        P(),
    )
    return jax.shard_map(
        per_device, mesh=mesh, in_specs=placed, out_specs=P(("seq", "head"), None), check_vma=False
    )
```

```python
import functools

import jax
import jax.numpy as jnp
from jax import lax
from jax.experimental import pallas as pl
from jax.experimental.pallas import tpu as pltpu
from jax.sharding import PartitionSpec as P

HEAD_DIM = 128
SPAN = 64
NBR_LEN = 64
K_NBR = 2
DB_DEV = 8
KEYS = K_NBR * NBR_LEN
SHARERS = 4
BLOCK_HEADS = 4
EXP_SCALE = HEAD_DIM ** (-0.5) * 1.4426950408889634


def xor_permute(x, bits):
    count = lax.axis_size("seq")
    return lax.ppermute(x, "seq", [(i, i ^ bits) for i in range(count)])


def shift_heads(x, shift):
    count = lax.axis_size("head")
    return lax.ppermute(x, "head", [(i, (i + shift) % count) for i in range(count)])


def after(x, *others):
    return lax.optimization_barrier((x, *others))[0]


def encode_kernel(raw_ref, w_ref, out_ref):
    values_in = raw_ref[...].astype(jnp.float32)
    mean_square = jnp.mean(values_in * values_in, axis=-1, keepdims=True)
    normed = (values_in * lax.rsqrt(mean_square + 1e-06)).astype(jnp.bfloat16)
    summed = jnp.dot(normed, w_ref[...], preferred_element_type=jnp.float32)
    out_ref[...] = (values_in + summed / (1.0 + jnp.exp(-summed))).astype(jnp.bfloat16)


def encode_rows(raw_rows, w_encoder):
    flops = 2 * raw_rows.size * w_encoder.shape[1]
    return pl.pallas_call(
        encode_kernel,
        out_shape=jax.ShapeDtypeStruct(raw_rows.shape, raw_rows.dtype),
        compiler_params=pltpu.CompilerParams(vmem_limit_bytes=24 << 20),
        cost_estimate=pl.CostEstimate(
            flops=flops, bytes_accessed=4 * raw_rows.size + 2 * w_encoder.size, transcendentals=raw_rows.size
        ),
        name="encode",
    )(raw_rows, w_encoder)


def attend_heads(keys_of, values_of, q_ref, o_ref, qf_ref, of_ref, offset):
    rows, wide = q_ref.shape
    spans = qf_ref.shape[0] // SPAN
    qf_ref[pl.ds(offset, rows), :] = q_ref[...]
    heads = [slice(at, at + HEAD_DIM) for at in range(0, wide, HEAD_DIM)]
    places = [(slice(span * SPAN, (span + 1) * SPAN), span, cols) for cols in heads for span in range(spans)]
    scores = [
        lax.dot_general(
            qf_ref[lines, cols], keys_of(span, cols), (((1,), (1,)), ((), ())), preferred_element_type=jnp.float32
        )
        for lines, span, cols in places
    ]
    probs = []
    for score in scores:
        highest = jnp.max(score, axis=-1, keepdims=True)
        raised = jnp.exp2(score * EXP_SCALE - highest * EXP_SCALE)
        probs.append((raised * (1.0 / jnp.sum(raised, axis=-1, keepdims=True))).astype(jnp.bfloat16))
    for (lines, span, cols), prob in zip(places, probs):
        mixed = jnp.dot(prob, values_of(span, cols), preferred_element_type=jnp.float32)
        of_ref[lines, cols] = mixed.astype(jnp.bfloat16)
    o_ref[...] = of_ref[pl.ds(offset, rows), :]


def span_rows(refs, span, cols):
    tokens = KEYS // len(refs)
    return jnp.concatenate([ref[span * tokens:(span + 1) * tokens, cols] for ref in refs], axis=0)


def make_parts(enc_refs, w, made_ref):
    for part, enc_ref in enumerate(enc_refs):
        made_ref[part] = jnp.dot(enc_ref[...], w, preferred_element_type=jnp.float32).astype(jnp.bfloat16)
    return [made_ref.at[part] for part in range(len(enc_refs))]


def own_kernel(parts, info_ref, *refs):
    enc_refs = refs[:parts - 1]
    first_k, first_v, wk_ref, wv_ref, q_ref, o_ref, ks_ref, vs_ref, qf_ref, of_ref = refs[parts - 1:]
    wide = q_ref.shape[1]
    here = pl.ds(pl.multiple_of(pl.program_id(0) * wide, wide), wide)
    k_refs = [first_k.at[:, here], *make_parts(enc_refs, wk_ref[:, here], ks_ref)]
    v_refs = [first_v.at[:, here], *make_parts(enc_refs, wv_ref[:, here], vs_ref)]
    attend_heads(
        functools.partial(span_rows, k_refs), functools.partial(span_rows, v_refs),
        q_ref, o_ref, qf_ref, of_ref, pl.multiple_of(info_ref[0], 16),
    )


def sent_kernel(parts, info_ref, *refs):
    enc_refs, wk_refs, wv_refs = refs[:parts], refs[parts:parts + SHARERS], refs[parts + SHARERS:parts + 2 * SHARERS]
    q_ref, _, o_ref, w_ref, sems, ks_ref, vs_ref, qf_ref, of_ref = refs[parts + 2 * SHARERS:]
    step = pl.program_id(0)
    slot = lax.rem(step, 2)

    def fetch(piece, into):
        return [
            pltpu.make_async_copy(source, w_ref.at[into, at], sems.at[into, at])
            for at, source in enumerate((wk_refs[piece], wv_refs[piece]))
        ]

    for piece in range(SHARERS):
        @pl.when(step == max(piece - 1, 0))
        def _(piece=piece):
            for copy in fetch(piece, piece % 2):
                copy.start()
    for copy in fetch(0, slot):
        copy.wait()
    k_refs = make_parts(enc_refs, w_ref[slot, 0], ks_ref)
    v_refs = make_parts(enc_refs, w_ref[slot, 1], vs_ref)
    attend_heads(
        functools.partial(span_rows, k_refs), functools.partial(span_rows, v_refs),
        q_ref, o_ref, qf_ref, of_ref, pl.multiple_of(info_ref[0], 16),
    )


def cost(encoded, rows, columns):
    made = sum(part.size for part in encoded)
    return pl.CostEstimate(
        flops=4 * made * columns + 4 * rows * KEYS * columns,
        bytes_accessed=2 * made + 4 * rows * columns + 4 * encoded[0].shape[1] * columns,
        transcendentals=rows * KEYS * columns // HEAD_DIM,
    )


def scratch(parts, part_rows, spans, wide):
    return [pltpu.VMEM((parts, part_rows, wide), jnp.bfloat16)] * 2 + [
        pltpu.VMEM((spans * SPAN, wide), jnp.bfloat16)
    ] * 2


def attend_own(info, encoded, first_keys, first_values, w_key, w_value, queries, spans):
    rows, columns = queries.shape[0], w_key.shape[1]
    part_rows, enc_width = encoded[0].shape
    wide = min(BLOCK_HEADS * HEAD_DIM, columns)
    whole = pl.BlockSpec(memory_space=pltpu.VMEM)
    block = pl.BlockSpec((rows, wide), lambda i, s: (0, s[1] * (columns // wide) + i))
    return pl.pallas_call(
        functools.partial(own_kernel, len(encoded) + 1),
        grid_spec=pltpu.PrefetchScalarGridSpec(
            num_scalar_prefetch=1,
            grid=(columns // wide,),
            in_specs=[whole] * (len(encoded) + 4) + [block],
            out_specs=block,
            scratch_shapes=scratch(len(encoded), part_rows, spans, wide),
        ),
        out_shape=jax.ShapeDtypeStruct(queries.shape, queries.dtype),
        compiler_params=pltpu.CompilerParams(vmem_limit_bytes=32 << 20),
        cost_estimate=cost(encoded, rows, columns),
        name="attend_own",
    )(info, *encoded, first_keys, first_values, w_key, w_value, queries)


def attend_sent(info, encoded, key_pieces, value_pieces, queries, out, spans):
    parts, rows = len(encoded), queries.shape[0]
    part_rows, enc_width = encoded[0].shape
    wide = key_pieces[0].shape[1]
    whole = pl.BlockSpec((part_rows, enc_width), lambda i, s: (0, 0))
    weights = pl.BlockSpec(memory_space=pl.ANY)
    block = pl.BlockSpec((rows, wide), lambda i, s: (0, s[1 + i]))
    return pl.pallas_call(
        functools.partial(sent_kernel, parts),
        grid_spec=pltpu.PrefetchScalarGridSpec(
            num_scalar_prefetch=1,
            grid=(SHARERS,),
            in_specs=[whole] * parts + [weights] * (2 * SHARERS) + [block, pl.BlockSpec(memory_space=pl.ANY)],
            out_specs=block,
            scratch_shapes=[
                pltpu.VMEM((2, 2, enc_width, wide), jnp.bfloat16), pltpu.SemaphoreType.DMA((2, 2)),
                *scratch(parts, part_rows, spans, wide),
            ],
        ),
        out_shape=jax.ShapeDtypeStruct(out.shape, out.dtype),
        input_output_aliases={parts + 2 * SHARERS + 2: 0},
        compiler_params=pltpu.CompilerParams(vmem_limit_bytes=40 << 20),
        cost_estimate=cost(encoded, rows, SHARERS * wide),
        name="attend_sent",
    )(info, *encoded, *key_pieces, *value_pieces, queries, out)


def project(rows, weights):
    return jnp.dot(rows, weights, preferred_element_type=jnp.float32).astype(jnp.bfloat16)


def per_device(queries, database_rows, w_encoder, w_key, w_value, neighbour_ids):
    seq_count, head_count = lax.axis_size("seq"), lax.axis_size("head")
    seq_index, head_index = lax.axis_index("seq"), lax.axis_index("head")
    rows, group_cols = queries.shape[0], w_key.shape[1]
    half = seq_count // 2

    top, order = [half, half // 2, half + half // 2], [0, half, half // 2, half + half // 2]
    enc_blocks = jnp.stack([w_encoder, *[xor_permute(w_encoder, bits) for bits in top]])
    top_blocks, bit = enc_blocks, half // 4
    while bit:
        enc_blocks = jnp.concatenate([enc_blocks, xor_permute(enc_blocks, bit)], axis=0)
        order = order + [m ^ bit for m in order]
        bit //= 2
    place = jnp.array([order.index(m) for m in range(seq_count)], jnp.int32)
    place = place[seq_index ^ jnp.arange(seq_count, dtype=jnp.int32)]
    w_full = enc_blocks[place].reshape(-1, w_encoder.shape[1])

    by_shard = neighbour_ids.reshape(seq_count, -1)
    cited_count = by_shard.shape[1]
    cap_count = max(2, (cited_count + seq_count - 1) // seq_count)
    owners = by_shard // DB_DEV
    local_entry = by_shard % DB_DEV
    position = jnp.arange(cited_count, dtype=jnp.int32)
    same_owner = (owners[:, :, None] == owners[:, None, :]) & (
        position[None, None, :] < position[None, :, None]
    )
    earlier = jnp.sum(same_owner.astype(jnp.int32), axis=2)
    slot_index = jnp.arange(cap_count, dtype=jnp.int32)
    matches = (owners == seq_index)[:, None, :] & (earlier[:, None, :] == slot_index[None, :, None])
    source_entry = jnp.sum(jnp.where(matches, local_entry[:, None, :], 0), axis=2)
    entries = after(database_rows[source_entry], top_blocks)
    arrived = lax.all_to_all(entries, "seq", split_axis=0, concat_axis=0, tiled=True)
    flat_arrived = arrived.reshape(-1, arrived.shape[2], arrived.shape[3])
    cited_slot = lax.dynamic_index_in_dim(owners * cap_count + earlier, seq_index, 0, keepdims=False)

    shard_spans = cited_count // K_NBR
    spans = max(-(-(h * rows % SPAN + rows) // SPAN) for h in range(head_count))

    def neighbours_of(head):
        first_span = head * rows // SPAN
        span_ids = jnp.minimum(first_span + jnp.arange(spans, dtype=jnp.int32), shard_spans - 1)
        places = (span_ids[:, None] * K_NBR + jnp.arange(K_NBR, dtype=jnp.int32)).reshape(-1)
        return flat_arrived[cited_slot[places]].reshape(-1, flat_arrived.shape[2])

    received = [
        shift_heads(neighbours_of((head_index + shift) % head_count), shift) for shift in range(1, head_count)
    ]
    kept = neighbours_of(head_index)

    encoded = [encode_rows(part, w_full) for part in (kept, *received)]
    own_keys, own_values = project(encoded[0], w_key), project(encoded[0], w_value)
    piece_cols = group_cols // SHARERS
    piece_index = ((seq_index >> 1) ^ (seq_index >> 2)) % 2 * 2 + seq_index % 2
    sent = []
    for shift in range(1, head_count):
        shared = []
        for weights, axis_bit in ((w_key, 4), (w_value, 2)):
            first = shift_heads(lax.dynamic_slice_in_dim(weights, piece_index * piece_cols, piece_cols, 1), shift)
            second = xor_permute(first, axis_bit)
            shared.append((first, second, xor_permute(first, 1), xor_permute(after(second, own_values), 1)))
        group = (head_index - shift) % head_count
        sent.append((shared, [group * SHARERS + (piece_index ^ mask) for mask in (0, 2, 1, 3)]))

    offset = head_index * rows % SPAN
    framed = rows % 16 != 0
    if framed:
        frame = jnp.zeros((spans * SPAN, queries.shape[1]), queries.dtype)
        queries = lax.dynamic_update_slice_in_dim(frame, queries, offset, 0)
        first_row, offset = offset, jnp.int32(0)
    info = jnp.stack([offset, head_index]).astype(jnp.int32)
    out = attend_own(info, encoded[1:], own_keys, own_values, w_key, w_value, queries, spans)
    for (key_pieces, value_pieces), blocks in sent:
        info = jnp.stack([offset, *blocks]).astype(jnp.int32)
        out = attend_sent(info, encoded, key_pieces, value_pieces, queries, out, spans)
    if framed:
        out = lax.dynamic_slice_in_dim(out, first_row, rows, 0)
    return out


def solution(mesh):
    placed = (
        P(("seq", "head"), None),
        P("seq", "head", None),
        P("seq", None),
        P(None, "head"),
        P(None, "head"),
        P(),
    )
    return jax.shard_map(
        per_device, mesh=mesh, in_specs=placed, out_specs=P(("seq", "head"), None), check_vma=False
    )
```

```python
import functools

import jax
import jax.numpy as jnp
from jax import lax
from jax.experimental import pallas as pl
from jax.experimental.pallas import tpu as pltpu
from jax.sharding import PartitionSpec as P

HEAD_DIM = 128
SPAN = 64
NBR_LEN = 64
K_NBR = 2
DB_DEV = 8
KEYS = K_NBR * NBR_LEN
SHARERS = 4
BLOCK_HEADS = 4
EXP_SCALE = HEAD_DIM ** (-0.5) * 1.4426950408889634


def xor_permute(x, bits):
    count = lax.axis_size("seq")
    return lax.ppermute(x, "seq", [(i, i ^ bits) for i in range(count)])


def shift_heads(x, shift):
    count = lax.axis_size("head")
    return lax.ppermute(x, "head", [(i, (i + shift) % count) for i in range(count)])


def after(x, *others):
    return lax.optimization_barrier((x, *others))[0]


def encode_kernel(raw_ref, w_ref, out_ref):
    values_in = raw_ref[...].astype(jnp.float32)
    mean_square = jnp.mean(values_in * values_in, axis=-1, keepdims=True)
    normed = (values_in * lax.rsqrt(mean_square + 1e-06)).astype(jnp.bfloat16)
    summed = jnp.dot(normed, w_ref[...], preferred_element_type=jnp.float32)
    out_ref[...] = (values_in + summed / (1.0 + jnp.exp(-summed))).astype(jnp.bfloat16)


def encode_rows(raw_rows, w_encoder):
    flops = 2 * raw_rows.size * w_encoder.shape[1]
    return pl.pallas_call(
        encode_kernel,
        out_shape=jax.ShapeDtypeStruct(raw_rows.shape, raw_rows.dtype),
        compiler_params=pltpu.CompilerParams(vmem_limit_bytes=24 << 20),
        cost_estimate=pl.CostEstimate(
            flops=flops, bytes_accessed=4 * raw_rows.size + 2 * w_encoder.size, transcendentals=raw_rows.size
        ),
        name="encode",
    )(raw_rows, w_encoder)


def attend_heads(keys_of, make_values, q_ref, o_ref, qf_ref, of_ref, offset):
    rows, wide = q_ref.shape
    spans = qf_ref.shape[0] // SPAN
    qf_ref[pl.ds(offset, rows), :] = q_ref[...]
    heads = [slice(at, at + HEAD_DIM) for at in range(0, wide, HEAD_DIM)]
    places = [(slice(span * SPAN, (span + 1) * SPAN), span, cols) for cols in heads for span in range(spans)]
    scores = [
        lax.dot_general(
            qf_ref[lines, cols], keys_of(span, cols), (((1,), (1,)), ((), ())), preferred_element_type=jnp.float32
        )
        for lines, span, cols in places
    ]
    values_of = make_values()
    probs = []
    for score in scores:
        highest = jnp.max(score, axis=-1, keepdims=True)
        raised = jnp.exp2(score * EXP_SCALE - highest * EXP_SCALE)
        probs.append((raised * (1.0 / jnp.sum(raised, axis=-1, keepdims=True))).astype(jnp.bfloat16))
    for (lines, span, cols), prob in zip(places, probs):
        mixed = jnp.dot(prob, values_of(span, cols), preferred_element_type=jnp.float32)
        of_ref[lines, cols] = mixed.astype(jnp.bfloat16)
    o_ref[...] = of_ref[pl.ds(offset, rows), :]


def span_rows(refs, span, cols):
    tokens = KEYS // len(refs)
    return jnp.concatenate([ref[span * tokens:(span + 1) * tokens, cols] for ref in refs], axis=0)


def make_parts(enc_refs, w, made_ref):
    for part, enc_ref in enumerate(enc_refs):
        made_ref[part] = jnp.dot(enc_ref[...], w, preferred_element_type=jnp.float32).astype(jnp.bfloat16)
    return [made_ref.at[part] for part in range(len(enc_refs))]


def own_kernel(parts, info_ref, *refs):
    enc_refs = refs[:parts - 1]
    first_k, first_v, wk_ref, wv_ref, q_ref, o_ref, ks_ref, vs_ref, qf_ref, of_ref = refs[parts - 1:]
    wide = q_ref.shape[1]
    here = pl.ds(pl.multiple_of(pl.program_id(0) * wide, wide), wide)
    k_refs = [first_k.at[:, here], *make_parts(enc_refs, wk_ref[:, here], ks_ref)]

    def make_values():
        v_refs = [first_v.at[:, here], *make_parts(enc_refs, wv_ref[:, here], vs_ref)]
        return functools.partial(span_rows, v_refs)

    attend_heads(
        functools.partial(span_rows, k_refs), make_values,
        q_ref, o_ref, qf_ref, of_ref, pl.multiple_of(info_ref[0], 16),
    )


def sent_kernel(parts, info_ref, *refs):
    enc_refs, wk_refs, wv_refs = refs[:parts], refs[parts:parts + SHARERS], refs[parts + SHARERS:parts + 2 * SHARERS]
    q_ref, _, o_ref, w_ref, sems, ks_ref, vs_ref, qf_ref, of_ref = refs[parts + 2 * SHARERS:]
    step = pl.program_id(0)
    slot = lax.rem(step, 2)

    def fetch(piece, into):
        return [
            pltpu.make_async_copy(source, w_ref.at[into, at], sems.at[into, at])
            for at, source in enumerate((wk_refs[piece], wv_refs[piece]))
        ]

    for piece in range(SHARERS):
        @pl.when(step == max(piece - 1, 0))
        def _(piece=piece):
            for copy in fetch(piece, piece % 2):
                copy.start()
    keys_here, values_here = fetch(0, slot)
    keys_here.wait()
    k_refs = make_parts(enc_refs, w_ref[slot, 0], ks_ref)

    def make_values():
        values_here.wait()
        return functools.partial(span_rows, make_parts(enc_refs, w_ref[slot, 1], vs_ref))

    attend_heads(
        functools.partial(span_rows, k_refs), make_values,
        q_ref, o_ref, qf_ref, of_ref, pl.multiple_of(info_ref[0], 16),
    )


def cost(encoded, rows, columns):
    made = sum(part.size for part in encoded)
    return pl.CostEstimate(
        flops=4 * made * columns + 4 * rows * KEYS * columns,
        bytes_accessed=2 * made + 4 * rows * columns + 4 * encoded[0].shape[1] * columns,
        transcendentals=rows * KEYS * columns // HEAD_DIM,
    )


def scratch(parts, part_rows, spans, wide):
    return [pltpu.VMEM((parts, part_rows, wide), jnp.bfloat16)] * 2 + [
        pltpu.VMEM((spans * SPAN, wide), jnp.bfloat16)
    ] * 2


def attend_own(info, encoded, first_keys, first_values, w_key, w_value, queries, spans):
    rows, columns = queries.shape[0], w_key.shape[1]
    part_rows, enc_width = encoded[0].shape
    wide = min(BLOCK_HEADS * HEAD_DIM, columns)
    whole = pl.BlockSpec(memory_space=pltpu.VMEM)
    block = pl.BlockSpec((rows, wide), lambda i, s: (0, s[1] * (columns // wide) + i))
    return pl.pallas_call(
        functools.partial(own_kernel, len(encoded) + 1),
        grid_spec=pltpu.PrefetchScalarGridSpec(
            num_scalar_prefetch=1,
            grid=(columns // wide,),
            in_specs=[whole] * (len(encoded) + 4) + [block],
            out_specs=block,
            scratch_shapes=scratch(len(encoded), part_rows, spans, wide),
        ),
        out_shape=jax.ShapeDtypeStruct(queries.shape, queries.dtype),
        compiler_params=pltpu.CompilerParams(vmem_limit_bytes=32 << 20),
        cost_estimate=cost(encoded, rows, columns),
        name="attend_own",
    )(info, *encoded, first_keys, first_values, w_key, w_value, queries)


def attend_sent(info, encoded, key_pieces, value_pieces, queries, out, spans):
    parts, rows = len(encoded), queries.shape[0]
    part_rows, enc_width = encoded[0].shape
    wide = key_pieces[0].shape[1]
    whole = pl.BlockSpec((part_rows, enc_width), lambda i, s: (0, 0))
    weights = pl.BlockSpec(memory_space=pl.ANY)
    block = pl.BlockSpec((rows, wide), lambda i, s: (0, s[1 + i]))
    return pl.pallas_call(
        functools.partial(sent_kernel, parts),
        grid_spec=pltpu.PrefetchScalarGridSpec(
            num_scalar_prefetch=1,
            grid=(SHARERS,),
            in_specs=[whole] * parts + [weights] * (2 * SHARERS) + [block, pl.BlockSpec(memory_space=pl.ANY)],
            out_specs=block,
            scratch_shapes=[
                pltpu.VMEM((2, 2, enc_width, wide), jnp.bfloat16), pltpu.SemaphoreType.DMA((2, 2)),
                *scratch(parts, part_rows, spans, wide),
            ],
        ),
        out_shape=jax.ShapeDtypeStruct(out.shape, out.dtype),
        input_output_aliases={parts + 2 * SHARERS + 2: 0},
        compiler_params=pltpu.CompilerParams(vmem_limit_bytes=40 << 20),
        cost_estimate=cost(encoded, rows, SHARERS * wide),
        name="attend_sent",
    )(info, *encoded, *key_pieces, *value_pieces, queries, out)


def project(rows, weights):
    return jnp.dot(rows, weights, preferred_element_type=jnp.float32).astype(jnp.bfloat16)


def per_device(queries, database_rows, w_encoder, w_key, w_value, neighbour_ids):
    seq_count, head_count = lax.axis_size("seq"), lax.axis_size("head")
    seq_index, head_index = lax.axis_index("seq"), lax.axis_index("head")
    rows, group_cols = queries.shape[0], w_key.shape[1]
    half = seq_count // 2

    top, order = [half, half // 2, half + half // 2], [0, half, half // 2, half + half // 2]
    enc_blocks = jnp.stack([w_encoder, *[xor_permute(w_encoder, bits) for bits in top]])
    top_blocks, bit = enc_blocks, half // 4
    while bit:
        enc_blocks = jnp.concatenate([enc_blocks, xor_permute(enc_blocks, bit)], axis=0)
        order = order + [m ^ bit for m in order]
        bit //= 2
    place = jnp.array([order.index(m) for m in range(seq_count)], jnp.int32)
    place = place[seq_index ^ jnp.arange(seq_count, dtype=jnp.int32)]
    w_full = enc_blocks[place].reshape(-1, w_encoder.shape[1])

    by_shard = neighbour_ids.reshape(seq_count, -1)
    cited_count = by_shard.shape[1]
    cap_count = max(2, (cited_count + seq_count - 1) // seq_count)
    owners = by_shard // DB_DEV
    local_entry = by_shard % DB_DEV
    position = jnp.arange(cited_count, dtype=jnp.int32)
    same_owner = (owners[:, :, None] == owners[:, None, :]) & (
        position[None, None, :] < position[None, :, None]
    )
    earlier = jnp.sum(same_owner.astype(jnp.int32), axis=2)
    slot_index = jnp.arange(cap_count, dtype=jnp.int32)
    matches = (owners == seq_index)[:, None, :] & (earlier[:, None, :] == slot_index[None, :, None])
    source_entry = jnp.sum(jnp.where(matches, local_entry[:, None, :], 0), axis=2)
    entries = after(database_rows[source_entry], top_blocks)
    arrived = lax.all_to_all(entries, "seq", split_axis=0, concat_axis=0, tiled=True)
    flat_arrived = arrived.reshape(-1, arrived.shape[2], arrived.shape[3])
    cited_slot = lax.dynamic_index_in_dim(owners * cap_count + earlier, seq_index, 0, keepdims=False)

    shard_spans = cited_count // K_NBR
    spans = max(-(-(h * rows % SPAN + rows) // SPAN) for h in range(head_count))

    def neighbours_of(head):
        first_span = head * rows // SPAN
        span_ids = jnp.minimum(first_span + jnp.arange(spans, dtype=jnp.int32), shard_spans - 1)
        places = (span_ids[:, None] * K_NBR + jnp.arange(K_NBR, dtype=jnp.int32)).reshape(-1)
        return flat_arrived[cited_slot[places]].reshape(-1, flat_arrived.shape[2])

    received = [
        shift_heads(neighbours_of((head_index + shift) % head_count), shift) for shift in range(1, head_count)
    ]
    kept = neighbours_of(head_index)

    encoded = [encode_rows(part, w_full) for part in (kept, *received)]
    own_keys, own_values = project(encoded[0], w_key), project(encoded[0], w_value)
    piece_cols = group_cols // SHARERS
    piece_index = ((seq_index >> 1) ^ (seq_index >> 2)) % 2 * 2 + seq_index % 2
    sent = []
    for shift in range(1, head_count):
        shared = []
        for weights, axis_bit in ((w_key, 2), (w_value, 4)):
            first = shift_heads(lax.dynamic_slice_in_dim(weights, piece_index * piece_cols, piece_cols, 1), shift)
            second = xor_permute(first, axis_bit)
            shared.append((first, second, xor_permute(first, 1), xor_permute(after(second, own_values), 1)))
        group = (head_index - shift) % head_count
        sent.append((shared, [group * SHARERS + (piece_index ^ mask) for mask in (0, 2, 1, 3)]))

    offset = head_index * rows % SPAN
    framed = rows % 16 != 0
    if framed:
        frame = jnp.zeros((spans * SPAN, queries.shape[1]), queries.dtype)
        queries = lax.dynamic_update_slice_in_dim(frame, queries, offset, 0)
        first_row, offset = offset, jnp.int32(0)
    info = jnp.stack([offset, head_index]).astype(jnp.int32)
    out = attend_own(info, encoded[1:], own_keys, own_values, w_key, w_value, queries, spans)
    for (key_pieces, value_pieces), blocks in sent:
        info = jnp.stack([offset, *blocks]).astype(jnp.int32)
        out = attend_sent(info, encoded, key_pieces, value_pieces, queries, out, spans)
    if framed:
        out = lax.dynamic_slice_in_dim(out, first_row, rows, 0)
    return out


def solution(mesh):
    placed = (
        P(("seq", "head"), None),
        P("seq", "head", None),
        P("seq", None),
        P(None, "head"),
        P(None, "head"),
        P(),
    )
    return jax.shard_map(
        per_device, mesh=mesh, in_specs=placed, out_specs=P(("seq", "head"), None), check_vma=False
    )
```
